32 devices in a mesh: ctx: 4 (over z), fsdp: 8 (over y, x, core).
Axes of the slice: x: 2, y: 2, z: 4, core: 2. Of those that a mesh axis runs over, the one named last changes fastest.
Arguments:
- tokens: bfloat16 [8, 1024, 1024], P('fsdp', 'ctx'), may hold values from -6 to 6
- w_qkv: bfloat16 [1024, 3072], P('fsdp'), may hold values from -0.1875 to 0.1875
- b_query: bfloat16 [1024], P('fsdp'), may hold values from -3 to 3
- b_value: bfloat16 [1024], P('fsdp'), may hold values from -3 to 3
- w_attn_out: bfloat16 [1024, 1024], P('fsdp'), may hold values from -3 to 3
- b_attn_out: bfloat16 [1024], P('fsdp'), may hold values from -3 to 3
- norm1_gain: bfloat16 [1024], P('fsdp'), may hold values from 0.5 to 1.5
- norm1_shift: bfloat16 [1024], P('fsdp'), may hold values from -3 to 3
- w_up: bfloat16 [1024, 4096], P('fsdp'), may hold values from -0.1875 to 0.1875
- b_up: bfloat16 [4096], P('fsdp'), may hold values from -3 to 3
- w_down: bfloat16 [4096, 1024], P('fsdp'), may hold values from -0.09375 to 0.09375
- b_down: bfloat16 [1024], P('fsdp'), may hold values from -3 to 3
- norm2_gain: bfloat16 [1024], P('fsdp'), may hold values from 0.5 to 1.5
- norm2_shift: bfloat16 [1024], P('fsdp'), may hold values from -3 to 3
- d_out: bfloat16 [8, 1024, 1024], P('fsdp', 'ctx'), may hold values from -6 to 6
Outputs:
- output: bfloat16 [8, 1024, 1024], P('fsdp', 'ctx')
- d_tokens: float32 [8, 1024, 1024], P('fsdp', 'ctx')
- grad_w_qkv: float32 [1024, 3072], P('fsdp')
- grad_b_query: float32 [1024], P('fsdp')
- grad_b_value: float32 [1024], P('fsdp')
- grad_w_attn_out: float32 [1024, 1024], P('fsdp')
- grad_b_attn_out: float32 [1024], P('fsdp')
- grad_norm1_gain: float32 [1024], P('fsdp')
- grad_norm1_shift: float32 [1024], P('fsdp')
- grad_w_up: float32 [1024, 4096], P('fsdp')
- grad_b_up: float32 [4096], P('fsdp')
- grad_w_down: float32 [4096, 1024], P('fsdp')
- grad_b_down: float32 [1024], P('fsdp')
- grad_norm2_gain: float32 [1024], P('fsdp')
- grad_norm2_shift: float32 [1024], P('fsdp')
The draws below stay inside these ranges and needn't reach their ends.
All inputs are finite; a program needn't handle non-finite values.
Results may differ from the reference program's by a relative error of at most 0.028.
Values may be sent and summed in bfloat16 or wider, within the bound.
A program may use at most 192 MiB of HBM per device.

```python
import jax
import jax.numpy as jnp
from jax import lax

D = 1024
HEADS = 16
HEAD_DIM = 64
FF = 4096
SEQ_LEN = 1024
SEQS = 8


def block_levels(stream_key, extent, pieces, smallest, high):
    level = 1.0
    for axis_at, blocks in pieces:
        heights = jax.random.uniform(jax.random.fold_in(jax.random.fold_in(stream_key, 6), axis_at), (blocks,), jnp.float32, smallest / len(pieces), high / len(pieces))
        level = level * jnp.repeat(jnp.exp(heights), extent[axis_at] // blocks).reshape((-1,) + (1,) * (len(extent) - 1 - axis_at))
    return level


def normal_values(rng, shape, spread, limit, pieces=(), dtype=jnp.bfloat16):
    drawn = spread * jax.random.normal(rng, shape, jnp.float32)
    if pieces:
        drawn = drawn * block_levels(rng, shape, pieces, -0.22, 0.18)
    return jnp.clip(drawn, -limit, limit).astype(dtype)


def setup_inputs(seed: int = 0) -> dict:
    splits = jax.random.split(jax.random.key(seed), 16)
    return {
        "tokens": normal_values(splits[0], (SEQS, SEQ_LEN, D), 1.0, 6.0, ((0, 8), (1, 4))),
        "w_qkv": normal_values(splits[1], (D, 3 * D), D ** -0.5, 0.1875, ((0, 8),)),
        "b_query": normal_values(splits[2], (D,), 0.5, 3.0, ((0, 8),)),
        "b_value": normal_values(splits[3], (D,), 0.5, 3.0, ((0, 8),)),
        "w_attn_out": normal_values(splits[4], (D, D), (max(1, D * 4 // SEQ_LEN)) ** -0.5, 3.0, ((0, 8),)),
        "b_attn_out": normal_values(splits[5], (D,), 0.5, 3.0, ((0, 8),)),
        "norm1_gain": jnp.clip(1.0 + 0.1 * jax.random.normal(splits[6], (D,), jnp.float32), 0.5, 1.5).astype(jnp.bfloat16),
        "norm1_shift": normal_values(splits[7], (D,), 0.5, 3.0, ((0, 8),)),
        "w_up": normal_values(splits[8], (D, FF), D ** -0.5, 0.1875, ((0, 8),)),
        "b_up": normal_values(splits[9], (FF,), 0.5, 3.0, ((0, 8),)),
        "w_down": normal_values(splits[10], (FF, D), FF ** -0.5, 0.09375, ((0, 8),)),
        "b_down": normal_values(splits[11], (D,), 0.5, 3.0, ((0, 8),)),
        "norm2_gain": jnp.clip(1.0 + 0.1 * jax.random.normal(splits[12], (D,), jnp.float32), 0.5, 1.5).astype(jnp.bfloat16),
        "norm2_shift": normal_values(splits[13], (D,), 0.5, 3.0, ((0, 8),)),
        "d_out": normal_values(splits[14], (SEQS, SEQ_LEN, D), 1.0, 6.0, ((0, 8), (1, 4))),
    }


@jax.custom_vjp
def low(v):
    return lax.optimization_barrier(v.astype(jnp.bfloat16)).astype(jnp.float32)

@jax.custom_vjp
def low_back(v):
    return v

def low_keep(v):
    return (low(v), None)

def low_pass(kept, grad):
    return (grad,)

def back_keep(v):
    return (v, None)

def back_low(kept, grad):
    return (low(grad),)
low.defvjp(low_keep, low_pass)
low_back.defvjp(back_keep, back_low)
norm_eps = 1e-05
highest = lax.Precision.HIGHEST

def matmul(first_op, second_op):
    return jnp.dot(first_op, second_op, precision=highest, preferred_element_type=jnp.float32)

def layer_norm(inputs, gain, shift):
    center = inputs - lax.optimization_barrier(jnp.mean(inputs, axis=-1, keepdims=True))
    variance = lax.optimization_barrier(jnp.mean(center * center, axis=-1, keepdims=True))
    return center * lax.rsqrt(variance + norm_eps) * gain + shift

def attend(triple):
    queries, key_vals, values = triple
    scores = low_back(jnp.einsum('qhd,khd->hqk', queries, key_vals, precision=highest) * HEAD_DIM ** (-0.5))
    attn_prob = jax.nn.softmax(scores, axis=-1)
    return jnp.einsum('hqk,khd->qhd', low(attn_prob), values, precision=highest)

def forward(tok_rows, w_qkv, b_query, b_value, w_attn_out, b_attn_out, norm1_gain, norm1_shift, w_up, b_up, w_down, b_down, norm2_gain, norm2_shift):
    proj_all = matmul(tok_rows, w_qkv)
    shaped = (SEQS, SEQ_LEN, HEADS, HEAD_DIM)
    queries = low_back(low(proj_all[:, :D] + b_query)).reshape(shaped)
    key_vals = low_back(low(proj_all[:, D:2 * D])).reshape(shaped)
    values = low_back(low(proj_all[:, 2 * D:] + b_value)).reshape(shaped)
    attended = lax.map(jax.checkpoint(attend), (queries, key_vals, values))
    attn_in = low_back(low(attended.reshape(SEQS * SEQ_LEN, D)))
    attn_out = low_back(matmul(attn_in, w_attn_out) + b_attn_out)
    normed = layer_norm(tok_rows + attn_out, norm1_gain, norm1_shift)
    hidden = low_back(matmul(low(normed), w_up) + b_up)
    activated = low(jax.nn.gelu(hidden, approximate=False))
    branch = low_back(matmul(activated, w_down) + b_down)
    return layer_norm(normed + branch, norm2_gain, norm2_shift)

def reference(tokens, w_qkv, b_query, b_value, w_attn_out, b_attn_out, norm1_gain, norm1_shift, w_up, b_up, w_down, b_down, norm2_gain, norm2_shift, d_out):
    params = tuple((item.astype(jnp.float32) for item in (w_qkv, b_query, b_value, w_attn_out, b_attn_out, norm1_gain, norm1_shift, w_up, b_up, w_down, b_down, norm2_gain, norm2_shift)))
    tok_rows = tokens.astype(jnp.float32).reshape(SEQS * SEQ_LEN, D)
    result, pull = jax.vjp(forward, tok_rows, *params)
    grads = pull(d_out.astype(jnp.float32).reshape(SEQS * SEQ_LEN, D))
    return (result.astype(jnp.bfloat16).reshape(SEQS, SEQ_LEN, D), grads[0].reshape(SEQS, SEQ_LEN, D), grads[1], grads[2], grads[3], grads[4], grads[5], grads[6], grads[7], grads[8], grads[9], grads[10], grads[11], grads[12], grads[13])
```

```python
import jax
import jax.numpy as jnp
from jax import lax
from jax.sharding import PartitionSpec as P

HEADS = 16
HEAD_DIM = 64


norm_eps = 1e-05


def layer_norm(inputs, gain, shift):
    center = inputs - jnp.mean(inputs, axis=-1, keepdims=True)
    variance = jnp.mean(center * center, axis=-1, keepdims=True)
    return center * lax.rsqrt(variance + norm_eps) * gain + shift


def gelu_exact(hidden):
    return jax.nn.gelu(hidden, approximate=False)


def swap(value, axis, mask):
    size = lax.axis_size(axis)
    return lax.ppermute(value, axis, [(at, at ^ mask) for at in range(size)])


def add(first, second):
    return (first.astype(jnp.float32) + second.astype(jnp.float32)).astype(jnp.bfloat16)


def bits_of(axis):
    return lax.axis_size(axis).bit_length() - 1


def two_ways(bits):
    outer = list(range(1, bits))
    return (outer + [0], outer[::-1] + [0])


def gather_half(shard, order):
    held, done = shard[None], []
    for bit in order:
        other = swap(held, "fsdp", 1 << bit)
        done.append(bit)
        lower = sum(1 for at in done if at < bit)
        rest = held.shape[1:]
        inner = 1 << lower
        split = (held.shape[0] // inner, 1, inner) + rest
        held = jnp.concatenate((held.reshape(split), other.reshape(split)), axis=1)
        held = held.reshape((-1,) + rest)
    return held


def gather(shard):
    half = shard.shape[1] // 2
    first, second = two_ways(bits_of("fsdp"))
    whole = jnp.concatenate(
        (gather_half(shard[:, :half], first), gather_half(shard[:, half:], second)), axis=2
    )
    return whole.reshape(-1, shard.shape[1])


def ctx_total(value):
    me = lax.axis_index("ctx")
    gray = me ^ (me >> 1)
    bits = bits_of("ctx")
    for at in range(bits):
        half = value.shape[0] // 2
        mine = (gray >> at) & 1
        keep = lax.dynamic_slice_in_dim(value, mine * half, half, 0)
        send = lax.dynamic_slice_in_dim(value, (1 - mine) * half, half, 0)
        value = add(keep, swap(send, "ctx", (2 << at) - 1))
    for at in reversed(range(bits)):
        other = swap(value, "ctx", (2 << at) - 1)
        upper = ((gray >> at) & 1) == 1
        value = jnp.concatenate(
            (jnp.where(upper, other, value), jnp.where(upper, value, other)), axis=0
        )
    return value.astype(jnp.float32)


def reduce_grad(grad):
    count = lax.axis_size("fsdp")
    columns = grad.shape[1]
    half = columns // 2
    blocks = grad.astype(jnp.bfloat16).reshape(count, -1, columns)
    pairs = blocks.reshape(count // 2, 2, -1, columns)
    blocks = add(pairs[:, 0], swap(pairs[:, 1], "fsdp", 1))
    first, second = two_ways(bits_of("fsdp"))
    first = [bit - 1 for bit in first[:-1]]
    second = [bit - 1 for bit in second[:-1]]
    return jnp.concatenate(
        (
            ctx_total(scatter_outer(blocks[:, :, :half], first)),
            ctx_total(scatter_outer(blocks[:, :, half:], second)),
        ),
        axis=1,
    )


def scatter_outer(blocks, order):
    left = sorted(order)
    for bit in order:
        inner = 1 << left.index(bit)
        left.remove(bit)
        rest = blocks.shape[1:]
        parts = blocks.reshape((blocks.shape[0] // (2 * inner), 2, inner) + rest)
        came = swap(parts[:, 1], "fsdp", 2 << bit)
        blocks = add(parts[:, 0], came).reshape((-1,) + rest)
    return blocks[0]


def gray_mask(index):
    mask, at = 0, 0
    while index >> at:
        if (index >> at) & 1:
            mask ^= (2 << at) - 1
        at += 1
    return mask


def gather_tokens(rows):
    held = rows[None]
    for at in reversed(range(bits_of("ctx"))):
        other = swap(held, "ctx", (2 << at) - 1)
        held = interleave(held, other)
    return held


def interleave(held, other):
    rest = held.shape[1:]
    return jnp.stack((held, other), axis=1).reshape((-1,) + rest)


def scatter_tokens(blocks):
    while blocks.shape[0] > 1:
        at = bits_of("ctx") - (blocks.shape[0].bit_length() - 1)
        parts = blocks.reshape((-1, 2) + blocks.shape[1:])
        blocks = add(parts[:, 0], swap(parts[:, 1], "ctx", (2 << at) - 1))
    return blocks[0]


def reorder(value, count):
    me = lax.axis_index("fsdp")
    width = value.shape[1] // count
    return jnp.concatenate(
        [lax.dynamic_slice_in_dim(value, (me ^ at) * width, width, 1) for at in range(count)],
        axis=1,
    )


def dot(first, second):
    return jnp.dot(first, second, preferred_element_type=jnp.float32)


def dot_rows(first, second):
    return lax.dot_general(
        first, second, (((0,), (0,)), ((), ())), preferred_element_type=jnp.float32
    )


def dot_back(first, second):
    return lax.dot_general(
        first, second, (((1,), (1,)), ((), ())), preferred_element_type=jnp.float32
    )


def per_device(
    tokens,
    w_qkv,
    b_query,
    b_value,
    w_attn_out,
    b_attn_out,
    norm1_gain,
    norm1_shift,
    w_up,
    b_up,
    w_down,
    b_down,
    norm2_gain,
    norm2_shift,
    d_out,
):
    count = lax.axis_size("fsdp")
    seq_local, block_rows, width = tokens.shape
    row_count = seq_local * block_rows
    tok_rows = tokens.reshape(row_count, width)
    vectors = (
        b_query,
        b_value,
        b_attn_out,
        norm1_gain,
        norm1_shift,
        b_up,
        b_down,
        norm2_gain,
        norm2_shift,
    )
    packed = lax.all_gather(jnp.concatenate(vectors), "fsdp", axis=0, tiled=False)
    spread, start = [], 0
    for item in vectors:
        size = item.shape[0]
        spread.append(packed[:, start : start + size].reshape(-1).astype(jnp.float32))
        start += size
    (
        query_bias,
        value_bias,
        out_bias,
        gain_one,
        shift_one,
        up_bias,
        down_bias,
        gain_two,
        shift_two,
    ) = spread
    input_proj = gather(w_qkv)
    token_blocks = gather_tokens(tok_rows)
    out_weight = gather(w_attn_out)
    up_weight = gather(w_up)
    down_weight = gather(w_down)
    ctx_count = token_blocks.shape[0]
    score_scale = HEAD_DIM ** (-0.5)
    all_rows = reorder(token_blocks.reshape(ctx_count * row_count, width), count)
    own_rows = all_rows[:row_count]
    key_rows = ctx_count * block_rows

    def by_sequence(value):
        parts = value.reshape(ctx_count, seq_local, block_rows, HEADS, HEAD_DIM)
        return parts.transpose(1, 3, 0, 2, 4).reshape(seq_local, HEADS, key_rows, HEAD_DIM)

    def by_block(value):
        parts = value.reshape(seq_local, HEADS, ctx_count, block_rows, HEAD_DIM)
        return parts.transpose(2, 0, 3, 1, 4).reshape(ctx_count * row_count, width)

    def heads(value):
        return value.reshape(seq_local, block_rows, HEADS, HEAD_DIM).transpose(0, 2, 1, 3)

    def joined(value):
        return value.transpose(0, 2, 1, 3).reshape(row_count, width)

    queries = heads((dot(own_rows, input_proj[:, :width]) + query_bias).astype(jnp.bfloat16))
    kv_all = dot(all_rows, input_proj[:, width:])
    key_part = by_sequence(kv_all[:, :width].astype(jnp.bfloat16))
    value_part = by_sequence((kv_all[:, width:] + value_bias).astype(jnp.bfloat16))
    scores = (
        jnp.einsum("shqd,shkd->shqk", queries, key_part, preferred_element_type=jnp.float32)
        * score_scale
    )
    attn_prob = jax.nn.softmax(scores, axis=-1).astype(jnp.bfloat16)
    mixed_out = jnp.einsum(
        "shqk,shkd->shqd", attn_prob, value_part, preferred_element_type=jnp.float32
    )
    mixed_rows = joined(mixed_out)
    attn_in = reorder(mixed_rows.astype(jnp.bfloat16), count)
    attn_out = dot(attn_in, out_weight) + out_bias
    resid_one = tok_rows.astype(jnp.float32) + attn_out
    normed = layer_norm(resid_one, gain_one, shift_one)
    normed_low = reorder(normed.astype(jnp.bfloat16), count)
    hidden = dot(normed_low, up_weight) + up_bias
    activated = reorder(gelu_exact(hidden).astype(jnp.bfloat16), count)
    branch = dot(activated, down_weight) + down_bias
    resid_two = normed + branch
    result = layer_norm(resid_two, gain_two, shift_two)
    output = result.astype(jnp.bfloat16).reshape(seq_local, block_rows, width)
    cotangent = d_out.reshape(row_count, width).astype(jnp.float32)
    norm_pull = jax.vjp(layer_norm, resid_two, gain_two, shift_two)[1]
    grad_resid_two, grad_gain_two, grad_shift_two = norm_pull(cotangent)
    grad_branch = grad_resid_two.astype(jnp.bfloat16)
    sum_down = reduce_grad(dot_rows(activated, grad_branch))
    grad_down_bias = jnp.sum(grad_branch.astype(jnp.float32), axis=0)
    grad_act = reorder(dot_back(grad_branch, down_weight), count)
    grad_hidden = jax.vjp(gelu_exact, hidden)[1](grad_act)[0].astype(jnp.bfloat16)
    sum_up = reduce_grad(dot_rows(normed_low, grad_hidden))
    grad_up_bias = jnp.sum(grad_hidden.astype(jnp.float32), axis=0)
    grad_normed = grad_resid_two + reorder(dot_back(grad_hidden, up_weight), count)
    norm_pull_one = jax.vjp(layer_norm, resid_one, gain_one, shift_one)[1]
    grad_resid_one, grad_gain_one, grad_shift_one = norm_pull_one(grad_normed)
    grad_attn = grad_resid_one.astype(jnp.bfloat16)
    sum_out = reduce_grad(dot_rows(attn_in, grad_attn))
    grad_out_bias = jnp.sum(grad_attn.astype(jnp.float32), axis=0)
    grad_mixed = reorder(dot_back(grad_attn, out_weight).astype(jnp.bfloat16), count)
    grad_heads = heads(grad_mixed)
    row_delta = jnp.sum(grad_heads.astype(jnp.float32) * mixed_out, axis=-1, keepdims=True)
    grad_prob = jnp.einsum(
        "shqd,shkd->shqk", grad_heads, value_part, preferred_element_type=jnp.float32
    )
    grad_score = (attn_prob.astype(jnp.float32) * (grad_prob - row_delta)).astype(jnp.bfloat16)
    grad_value = jnp.einsum(
        "shqk,shqd->shkd", attn_prob, grad_heads, preferred_element_type=jnp.float32
    )
    grad_key = (
        jnp.einsum("shqk,shqd->shkd", grad_score, queries, preferred_element_type=jnp.float32)
        * score_scale
    )
    grad_query = (
        jnp.einsum("shqk,shkd->shqd", grad_score, key_part, preferred_element_type=jnp.float32)
        * score_scale
    )
    grad_queries = joined(grad_query).astype(jnp.bfloat16)
    grad_keys = by_block(grad_key).astype(jnp.bfloat16)
    grad_values = by_block(grad_value).astype(jnp.bfloat16)
    grad_kv = jnp.concatenate((grad_keys, grad_values), axis=1)
    grad_input_proj = jnp.concatenate(
        (dot_rows(own_rows, grad_queries), dot_rows(all_rows, grad_kv)), axis=1
    )
    sum_input = reduce_grad(grad_input_proj)
    grad_query_bias = jnp.sum(grad_queries.astype(jnp.float32), axis=0)
    grad_value_bias = jnp.sum(grad_values.astype(jnp.float32), axis=0)
    from_kv = dot_back(grad_kv, input_proj[:, width:])
    from_query = dot_back(grad_queries, input_proj[:, :width])
    from_kv = scatter_tokens(from_kv.astype(jnp.bfloat16).reshape(ctx_count, row_count, width))
    d_tokens = grad_resid_one + reorder(from_query + from_kv.astype(jnp.float32), count)
    small = (
        grad_query_bias,
        grad_value_bias,
        grad_out_bias,
        grad_gain_one,
        grad_shift_one,
        grad_up_bias,
        grad_down_bias,
        grad_gain_two,
        grad_shift_two,
    )
    small_all = lax.psum(
        jnp.concatenate([item.reshape(count, -1) for item in small], axis=1), ("fsdp", "ctx")
    )
    small_own = lax.dynamic_index_in_dim(small_all, lax.axis_index("fsdp"), 0, keepdims=False)
    owned, start = [], 0
    for item in small:
        size = item.shape[0] // count
        owned.append(small_own[start : start + size])
        start += size
    return (
        output,
        d_tokens.reshape(seq_local, block_rows, width),
        sum_input,
        owned[0],
        owned[1],
        sum_out,
        owned[2],
        owned[3],
        owned[4],
        sum_up,
        owned[5],
        sum_down,
        owned[6],
        owned[7],
        owned[8],
    )


def solution(mesh):
    placed = (
        P("fsdp", "ctx", None),
        P("fsdp", None),
        P("fsdp"),
        P("fsdp"),
        P("fsdp", None),
        P("fsdp"),
        P("fsdp"),
        P("fsdp"),
        P("fsdp", None),
        P("fsdp"),
        P("fsdp", None),
        P("fsdp"),
        P("fsdp"),
        P("fsdp"),
        P("fsdp", "ctx", None),
    )
    return jax.shard_map(
        per_device,
        mesh=mesh,
        in_specs=placed,
        out_specs=(
            P("fsdp", "ctx", None),
            P("fsdp", "ctx", None),
            P("fsdp", None),
            P("fsdp"),
            P("fsdp"),
            P("fsdp", None),
            P("fsdp"),
            P("fsdp"),
            P("fsdp"),
            P("fsdp", None),
            P("fsdp"),
            P("fsdp", None),
            P("fsdp"),
            P("fsdp"),
            P("fsdp"),
        ),
        check_vma=False,
    )
```

```python
import jax
import jax.numpy as jnp
from jax import lax
from jax.sharding import PartitionSpec as P

HEADS = 16
HEAD_DIM = 64


norm_eps = 1e-05


def layer_norm(inputs, gain, shift):
    center = inputs - jnp.mean(inputs, axis=-1, keepdims=True)
    variance = jnp.mean(center * center, axis=-1, keepdims=True)
    return center * lax.rsqrt(variance + norm_eps) * gain + shift


def gelu_exact(hidden):
    return jax.nn.gelu(hidden, approximate=False)


def swap(value, axis, mask):
    size = lax.axis_size(axis)
    return lax.ppermute(value, axis, [(at, at ^ mask) for at in range(size)])


def add(first, second):
    return (first.astype(jnp.float32) + second.astype(jnp.float32)).astype(jnp.bfloat16)


def bits_of(axis):
    return lax.axis_size(axis).bit_length() - 1


def two_ways(bits):
    outer = list(range(1, bits))
    return (outer + [0], outer[::-1] + [0])


def tie(*values):
    return lax.optimization_barrier(values)


def halves(value):
    middle = value.shape[-1] // 256 * 128
    return value[..., :middle], value[..., middle:]


def gather_hop(held, bit, done):
    other = swap(held, "fsdp", 1 << bit)
    inner = 1 << sum(1 for at in done if at < bit)
    rest = held.shape[1:]
    split = (held.shape[0] // inner, 1, inner) + rest
    held = jnp.concatenate((held.reshape(split), other.reshape(split)), axis=1)
    return held.reshape((-1,) + rest)


def gather_hops(pair, first, last):
    moved = []
    for held, order in zip(pair, two_ways(bits_of("fsdp"))):
        for at in range(first, last):
            held = gather_hop(held, order[at], order[:at])
        moved.append(held)
    return tuple(moved)


def whole(pair):
    joined = jnp.concatenate(pair, axis=2)
    return joined.reshape(-1, joined.shape[2])


def ctx_hops(value, first, last):
    me = lax.axis_index("ctx")
    gray = me ^ (me >> 1)
    bits = bits_of("ctx")
    for hop in range(first, last):
        if hop < bits:
            half = value.shape[1] // 2
            mine = (gray >> hop) & 1
            keep = lax.dynamic_slice_in_dim(value, mine * half, half, 1)
            send = lax.dynamic_slice_in_dim(value, (1 - mine) * half, half, 1)
            value = add(keep, swap(send, "ctx", (2 << hop) - 1))
        else:
            at = 2 * bits - 1 - hop
            other = swap(value, "ctx", (2 << at) - 1)
            upper = ((gray >> at) & 1) == 1
            value = jnp.concatenate(
                (jnp.where(upper, other, value), jnp.where(upper, value, other)), axis=1
            )
    return value


def as_blocks(grad):
    return grad.astype(jnp.bfloat16).reshape(lax.axis_size("fsdp"), -1, grad.shape[1])


def scatter_core(blocks):
    pairs = blocks.reshape((-1, 2) + blocks.shape[1:])
    return halves(add(pairs[:, 0], swap(pairs[:, 1], "fsdp", 1)))


def scatter_hops(pair, first, last):
    moved = []
    for blocks, order in zip(pair, two_ways(bits_of("fsdp"))):
        for at in range(first, last):
            inner = 1 << sorted(order[at:-1]).index(order[at])
            rest = blocks.shape[1:]
            parts = blocks.reshape((blocks.shape[0] // (2 * inner), 2, inner) + rest)
            came = swap(parts[:, 1], "fsdp", 1 << order[at])
            blocks = add(parts[:, 0], came).reshape((-1,) + rest)
        moved.append(blocks)
    return tuple(moved)


def fold(value, width):
    return jnp.concatenate(
        [value[:, at : at + width] for at in range(0, value.shape[1], width)], axis=0
    )


def unfold(value, rows):
    return jnp.concatenate(
        [value[at : at + rows] for at in range(0, value.shape[0], rows)], axis=1
    )


def gray_mask(index):
    mask, at = 0, 0
    while index >> at:
        if (index >> at) & 1:
            mask ^= (2 << at) - 1
        at += 1
    return mask


def gather_tokens(rows):
    held = rows[None]
    for at in reversed(range(bits_of("ctx"))):
        other = swap(held, "ctx", (2 << at) - 1)
        held = interleave(held, other)
    return held


def interleave(held, other):
    rest = held.shape[1:]
    return jnp.stack((held, other), axis=1).reshape((-1,) + rest)


def scatter_tokens(blocks):
    while blocks.shape[0] > 1:
        at = bits_of("ctx") - (blocks.shape[0].bit_length() - 1)
        parts = blocks.reshape((-1, 2) + blocks.shape[1:])
        blocks = add(parts[:, 0], swap(parts[:, 1], "ctx", (2 << at) - 1))
    return blocks[0]


def reorder(value, count):
    me = lax.axis_index("fsdp")
    width = value.shape[1] // count
    return jnp.concatenate(
        [lax.dynamic_slice_in_dim(value, (me ^ at) * width, width, 1) for at in range(count)],
        axis=1,
    )


def dot(first, second):
    return jnp.dot(first, second, preferred_element_type=jnp.float32)


def dot_rows(first, second):
    return lax.dot_general(
        first, second, (((0,), (0,)), ((), ())), preferred_element_type=jnp.float32
    )


def dot_back(first, second):
    return lax.dot_general(
        first, second, (((1,), (1,)), ((), ())), preferred_element_type=jnp.float32
    )


def per_device(
    tokens,
    w_qkv,
    b_query,
    b_value,
    w_attn_out,
    b_attn_out,
    norm1_gain,
    norm1_shift,
    w_up,
    b_up,
    w_down,
    b_down,
    norm2_gain,
    norm2_shift,
    d_out,
):
    count = lax.axis_size("fsdp")
    seq_local, block_rows, width = tokens.shape
    row_count = seq_local * block_rows
    tok_rows = tokens.reshape(row_count, width)
    vectors = (
        b_query,
        b_value,
        b_attn_out,
        norm1_gain,
        norm1_shift,
        b_up,
        b_down,
        norm2_gain,
        norm2_shift,
    )
    packed = lax.all_gather(jnp.concatenate(vectors), "fsdp", axis=0, tiled=False)
    spread, start = [], 0
    for item in vectors:
        size = item.shape[0]
        spread.append(packed[:, start : start + size].reshape(-1).astype(jnp.float32))
        start += size
    (
        query_bias,
        value_bias,
        out_bias,
        gain_one,
        shift_one,
        up_bias,
        down_bias,
        gain_two,
        shift_two,
    ) = spread
    bits = bits_of("fsdp")
    outer = bits - 1
    input_half = gather_hops(halves(w_qkv[None]), 0, outer)
    input_half, up_half, down_half = tie(
        input_half, halves(jnp.concatenate((w_attn_out, w_up), axis=1)[None]), halves(w_down[None])
    )
    input_proj = whole(gather_hops(input_half, outer, bits))
    token_blocks = gather_tokens(tok_rows)
    up_half = gather_hops(up_half, 0, outer)
    down_half = gather_hops(down_half, 0, outer)
    ctx_count = token_blocks.shape[0]
    score_scale = HEAD_DIM ** (-0.5)
    all_rows = reorder(token_blocks.reshape(ctx_count * row_count, width), count)
    own_rows = all_rows[:row_count]
    key_rows = ctx_count * block_rows

    def by_sequence(value):
        parts = value.reshape(ctx_count, seq_local, block_rows, HEADS, HEAD_DIM)
        return parts.transpose(1, 3, 0, 2, 4).reshape(seq_local, HEADS, key_rows, HEAD_DIM)

    def by_block(value):
        parts = value.reshape(seq_local, HEADS, ctx_count, block_rows, HEAD_DIM)
        return parts.transpose(2, 0, 3, 1, 4).reshape(ctx_count * row_count, width)

    def heads(value):
        return value.reshape(seq_local, block_rows, HEADS, HEAD_DIM).transpose(0, 2, 1, 3)

    def joined(value):
        return value.transpose(0, 2, 1, 3).reshape(row_count, width)

    queries = heads((dot(own_rows, input_proj[:, :width]) + query_bias).astype(jnp.bfloat16))
    kv_all = dot(all_rows, input_proj[:, width:])
    key_part = by_sequence(kv_all[:, :width].astype(jnp.bfloat16))
    value_part = by_sequence((kv_all[:, width:] + value_bias).astype(jnp.bfloat16))
    scores = (
        jnp.einsum("shqd,shkd->shqk", queries, key_part, preferred_element_type=jnp.float32)
        * score_scale
    )
    attn_prob = jax.nn.softmax(scores, axis=-1).astype(jnp.bfloat16)
    up_half, down_half, attn_prob = tie(up_half, down_half, attn_prob)
    out_up = whole(gather_hops(up_half, outer, bits))
    down_weight = whole(gather_hops(down_half, outer, bits))
    out_weight, up_weight = out_up[:, :width], out_up[:, width:]
    mixed_out = jnp.einsum(
        "shqk,shkd->shqd", attn_prob, value_part, preferred_element_type=jnp.float32
    )
    mixed_rows = joined(mixed_out)
    attn_in = reorder(mixed_rows.astype(jnp.bfloat16), count)
    attn_out = dot(attn_in, out_weight) + out_bias
    resid_one = tok_rows.astype(jnp.float32) + attn_out
    normed = layer_norm(resid_one, gain_one, shift_one)
    normed_low = reorder(normed.astype(jnp.bfloat16), count)
    hidden = dot(normed_low, up_weight) + up_bias
    activated = reorder(gelu_exact(hidden).astype(jnp.bfloat16), count)
    branch = dot(activated, down_weight) + down_bias
    resid_two = normed + branch
    result = layer_norm(resid_two, gain_two, shift_two)
    output = result.astype(jnp.bfloat16).reshape(seq_local, block_rows, width)
    cotangent = d_out.reshape(row_count, width).astype(jnp.float32)
    norm_pull = jax.vjp(layer_norm, resid_two, gain_two, shift_two)[1]
    grad_resid_two, grad_gain_two, grad_shift_two = norm_pull(cotangent)
    grad_branch = grad_resid_two.astype(jnp.bfloat16)
    down_blocks, grad_branch = tie(as_blocks(dot_rows(activated, grad_branch)), grad_branch)
    down_pair = scatter_core(down_blocks)
    grad_down_bias = jnp.sum(grad_branch.astype(jnp.float32), axis=0)
    grad_act = reorder(dot_back(grad_branch, down_weight), count)
    grad_hidden = jax.vjp(gelu_exact, hidden)[1](grad_act)[0].astype(jnp.bfloat16)
    up_blocks, grad_hidden = tie(as_blocks(dot_rows(normed_low, grad_hidden)), grad_hidden)
    up_pair = scatter_core(up_blocks)
    grad_up_bias = jnp.sum(grad_hidden.astype(jnp.float32), axis=0)
    down_pair, grad_hidden = tie(down_pair, grad_hidden)
    down_pair = scatter_hops(down_pair, 0, 1)
    grad_normed = grad_resid_two + reorder(dot_back(grad_hidden, up_weight), count)
    norm_pull_one = jax.vjp(layer_norm, resid_one, gain_one, shift_one)[1]
    grad_resid_one, grad_gain_one, grad_shift_one = norm_pull_one(grad_normed)
    grad_attn = grad_resid_one.astype(jnp.bfloat16)
    grad_out_weight = dot_rows(attn_in, grad_attn)
    up_pair, grad_attn = tie(up_pair, grad_attn)
    up_pair = scatter_hops(up_pair, 0, 1)
    grad_out_bias = jnp.sum(grad_attn.astype(jnp.float32), axis=0)
    grad_mixed = reorder(dot_back(grad_attn, out_weight).astype(jnp.bfloat16), count)
    grad_heads = heads(grad_mixed)
    row_delta = jnp.sum(grad_heads.astype(jnp.float32) * mixed_out, axis=-1, keepdims=True)
    grad_prob = jnp.einsum(
        "shqd,shkd->shqk", grad_heads, value_part, preferred_element_type=jnp.float32
    )
    grad_score = (attn_prob.astype(jnp.float32) * (grad_prob - row_delta)).astype(jnp.bfloat16)
    down_pair, grad_score = tie(down_pair, grad_score)
    down_pair = scatter_hops(down_pair, 1, outer)
    grad_value = jnp.einsum(
        "shqk,shqd->shkd", attn_prob, grad_heads, preferred_element_type=jnp.float32
    )
    grad_key = (
        jnp.einsum("shqk,shqd->shkd", grad_score, queries, preferred_element_type=jnp.float32)
        * score_scale
    )
    grad_query = (
        jnp.einsum("shqk,shkd->shqd", grad_score, key_part, preferred_element_type=jnp.float32)
        * score_scale
    )
    grad_queries = joined(grad_query).astype(jnp.bfloat16)
    grad_keys = by_block(grad_key).astype(jnp.bfloat16)
    grad_values = by_block(grad_value).astype(jnp.bfloat16)
    grad_kv = jnp.concatenate((grad_keys, grad_values), axis=1)
    up_pair, grad_kv = tie(up_pair, grad_kv)
    up_pair = scatter_hops(up_pair, 1, outer)
    grad_input_proj = jnp.concatenate(
        (dot_rows(own_rows, grad_queries), dot_rows(all_rows, grad_kv)), axis=1
    )
    grad_query_bias = jnp.sum(grad_queries.astype(jnp.float32), axis=0)
    grad_value_bias = jnp.sum(grad_values.astype(jnp.float32), axis=0)
    small = (
        grad_query_bias,
        grad_value_bias,
        grad_out_bias,
        grad_gain_one,
        grad_shift_one,
        grad_up_bias,
        grad_down_bias,
        grad_gain_two,
        grad_shift_two,
    )
    small_rows = jnp.concatenate([item.reshape(count, -1) for item in small], axis=1)
    small_size = small_rows.shape[1]
    me = lax.axis_index("fsdp")
    small_rows = jnp.concatenate(
        [lax.dynamic_slice_in_dim(small_rows, me ^ at, 1, 0) for at in range(count)], axis=0
    )
    own_width = width // count
    small_lines = -(-small_size // 128)
    small_rows = jnp.pad(small_rows, ((0, 0), (0, small_lines * 128 - small_size)))
    small_rows = small_rows.reshape(count, small_lines, 128).astype(jnp.bfloat16)
    small_rows = jnp.pad(small_rows, ((0, 0), (0, own_width - small_lines), (0, 0)))
    input_blocks = jnp.concatenate(
        (as_blocks(grad_input_proj), as_blocks(grad_out_weight), small_rows), axis=2
    )
    input_blocks, grad_kv = tie(input_blocks, grad_kv)
    input_pair = scatter_core(input_blocks)
    from_kv = dot_back(grad_kv, input_proj[:, width:])
    from_query = dot_back(grad_queries, input_proj[:, :width])
    input_pair, from_kv = tie(input_pair, from_kv)
    input_pair = scatter_hops(input_pair, 0, 1)
    from_kv = scatter_tokens(from_kv.astype(jnp.bfloat16).reshape(ctx_count, row_count, width))
    d_tokens = grad_resid_one + reorder(from_query + from_kv.astype(jnp.float32), count)
    down_own = jnp.concatenate(down_pair, axis=2)[0]
    up_own = jnp.concatenate(up_pair, axis=2)[0]
    first_group = jnp.concatenate((down_own, fold(up_own, width)), axis=0)
    ctx_steps = 2 * bits_of("ctx")
    first_group = ctx_hops(first_group, 0, 1)
    input_pair, first_group = tie(input_pair, first_group)
    input_pair = scatter_hops(input_pair, 1, outer)
    first_group = ctx_hops(first_group, 1, 2)
    input_pair, first_group = tie(input_pair, first_group)
    input_own = jnp.concatenate(input_pair, axis=2)[0]
    extra = input_own[:small_lines, 4 * width :].reshape(-1)
    extra = jnp.pad(extra, (0, -extra.shape[0] % (16 * width))).reshape(-1, width)
    second_group = jnp.concatenate((fold(input_own[:, : 4 * width], width), extra), axis=0)
    for step in range(2, ctx_steps):
        second_group = ctx_hops(second_group, step - 2, step - 1)
        first_group = ctx_hops(first_group, step, step + 1)
        first_group, second_group = tie(first_group, second_group)
    second_group = ctx_hops(second_group, ctx_steps - 2, ctx_steps)
    first_group = first_group.astype(jnp.float32)
    second_group = second_group.astype(jnp.float32)
    down_rows = down_own.shape[0]
    sum_down = first_group[:down_rows]
    sum_up = unfold(first_group[down_rows:], own_width)
    sum_input = unfold(second_group[: 3 * own_width], own_width)
    sum_out = second_group[3 * own_width : 4 * own_width]
    small_own = second_group[4 * own_width :].reshape(-1)
    owned, start = [], 0
    for item in small:
        size = item.shape[0] // count
        owned.append(small_own[start : start + size])
        start += size
    return (
        output,
        d_tokens.reshape(seq_local, block_rows, width),
        sum_input,
        owned[0],
        owned[1],
        sum_out,
        owned[2],
        owned[3],
        owned[4],
        sum_up,
        owned[5],
        sum_down,
        owned[6],
        owned[7],
        owned[8],
    )


def solution(mesh):
    placed = (
        P("fsdp", "ctx", None),
        P("fsdp", None),
        P("fsdp"),
        P("fsdp"),
        P("fsdp", None),
        P("fsdp"),
        P("fsdp"),
        P("fsdp"),
        P("fsdp", None),
        P("fsdp"),
        P("fsdp", None),
        P("fsdp"),
        P("fsdp"),
        P("fsdp"),
        P("fsdp", "ctx", None),
    )
    return jax.shard_map(
        per_device,
        mesh=mesh,
        in_specs=placed,
        out_specs=(
            P("fsdp", "ctx", None),
            P("fsdp", "ctx", None),
            P("fsdp", None),
            P("fsdp"),
            P("fsdp"),
            P("fsdp", None),
            P("fsdp"),
            P("fsdp"),
            P("fsdp"),
            P("fsdp", None),
            P("fsdp"),
            P("fsdp", None),
            P("fsdp"),
            P("fsdp"),
            P("fsdp"),
        ),
        check_vma=False,
    )
```

```python
import jax
import jax.numpy as jnp
from jax import lax
from jax.experimental import pallas as pl
from jax.experimental.pallas import tpu as pltpu
from jax.sharding import PartitionSpec as P

HEADS = 16
HEAD_DIM = 64


norm_eps = 1e-05


def layer_norm(inputs, gain, shift):
    center = inputs - jnp.mean(inputs, axis=-1, keepdims=True)
    variance = jnp.mean(center * center, axis=-1, keepdims=True)
    return center * lax.rsqrt(variance + norm_eps) * gain + shift


def gelu_exact(hidden):
    return jax.nn.gelu(hidden, approximate=False)


def swap(value, axis, mask):
    size = lax.axis_size(axis)
    return lax.ppermute(value, axis, [(at, at ^ mask) for at in range(size)])


def add(first, second):
    return (first.astype(jnp.float32) + second.astype(jnp.float32)).astype(jnp.bfloat16)


def bits_of(axis):
    return lax.axis_size(axis).bit_length() - 1


def two_ways(bits):
    outer = list(range(1, bits))
    return (outer + [0], outer[::-1] + [0])


def tie(*values):
    return lax.optimization_barrier(values)


def halves(value):
    middle = value.shape[-1] // 256 * 128
    return value[..., :middle], value[..., middle:]


def gather_hop(held, bit, done):
    other = swap(held, "fsdp", 1 << bit)
    inner = 1 << sum(1 for at in done if at < bit)
    rest = held.shape[1:]
    split = (held.shape[0] // inner, 1, inner) + rest
    held = jnp.concatenate((held.reshape(split), other.reshape(split)), axis=1)
    return held.reshape((-1,) + rest)


def gather_hops(pair, first, last):
    moved = []
    for held, order in zip(pair, two_ways(bits_of("fsdp"))):
        for at in range(first, last):
            held = gather_hop(held, order[at], order[:at])
        moved.append(held)
    return tuple(moved)


def whole(pair):
    joined = jnp.concatenate(pair, axis=2)
    return joined.reshape(-1, joined.shape[2])


def ctx_hops(value, first, last):
    me = lax.axis_index("ctx")
    gray = me ^ (me >> 1)
    bits = bits_of("ctx")
    for hop in range(first, last):
        if hop < bits:
            half = value.shape[1] // 2
            mine = (gray >> hop) & 1
            keep = lax.dynamic_slice_in_dim(value, mine * half, half, 1)
            send = lax.dynamic_slice_in_dim(value, (1 - mine) * half, half, 1)
            value = add(keep, swap(send, "ctx", (2 << hop) - 1))
        else:
            at = 2 * bits - 1 - hop
            other = swap(value, "ctx", (2 << at) - 1)
            upper = ((gray >> at) & 1) == 1
            value = jnp.concatenate(
                (jnp.where(upper, other, value), jnp.where(upper, value, other)), axis=1
            )
    return value


def as_blocks(grad):
    return grad.astype(jnp.bfloat16).reshape(lax.axis_size("fsdp"), -1, grad.shape[1])


def scatter_core(blocks):
    pairs = blocks.reshape((-1, 2) + blocks.shape[1:])
    return halves(add(pairs[:, 0], swap(pairs[:, 1], "fsdp", 1)))


def scatter_hops(pair, first, last):
    moved = []
    for blocks, order in zip(pair, two_ways(bits_of("fsdp"))):
        for at in range(first, last):
            inner = 1 << sorted(order[at:-1]).index(order[at])
            rest = blocks.shape[1:]
            parts = blocks.reshape((blocks.shape[0] // (2 * inner), 2, inner) + rest)
            came = swap(parts[:, 1], "fsdp", 1 << order[at])
            blocks = add(parts[:, 0], came).reshape((-1,) + rest)
        moved.append(blocks)
    return tuple(moved)


def fold(value, width):
    return jnp.concatenate(
        [value[:, at : at + width] for at in range(0, value.shape[1], width)], axis=0
    )


def unfold(value, rows):
    return jnp.concatenate(
        [value[at : at + rows] for at in range(0, value.shape[0], rows)], axis=1
    )


def gray_mask(index):
    mask, at = 0, 0
    while index >> at:
        if (index >> at) & 1:
            mask ^= (2 << at) - 1
        at += 1
    return mask


def gather_tokens(rows):
    held = rows[None]
    for at in reversed(range(bits_of("ctx"))):
        other = swap(held, "ctx", (2 << at) - 1)
        held = interleave(held, other)
    return held


def interleave(held, other):
    rest = held.shape[1:]
    return jnp.stack((held, other), axis=1).reshape((-1,) + rest)


def scatter_tokens(blocks):
    while blocks.shape[0] > 1:
        at = bits_of("ctx") - (blocks.shape[0].bit_length() - 1)
        parts = blocks.reshape((-1, 2) + blocks.shape[1:])
        blocks = add(parts[:, 0], swap(parts[:, 1], "ctx", (2 << at) - 1))
    return blocks[0]


def reorder(value, count):
    me = lax.axis_index("fsdp")
    width = value.shape[1] // count
    return jnp.concatenate(
        [lax.dynamic_slice_in_dim(value, (me ^ at) * width, width, 1) for at in range(count)],
        axis=1,
    )


def dot(first, second):
    return jnp.dot(first, second, preferred_element_type=jnp.float32)


def dot_rows(first, second):
    return lax.dot_general(
        first, second, (((0,), (0,)), ((), ())), preferred_element_type=jnp.float32
    )


def dot_back(first, second):
    return lax.dot_general(
        first, second, (((1,), (1,)), ((), ())), preferred_element_type=jnp.float32
    )


LANES = 128


def head_mask(head):
    lane = lax.broadcasted_iota(jnp.int32, (1, LANES), 1)
    return jnp.where(lane // HEAD_DIM == head, 1.0, 0.0).astype(jnp.float32)


def attend_kernel(q_ref, k_ref, v_ref, o_ref):
    queries = q_ref[0].astype(jnp.float32) * HEAD_DIM ** (-0.5)
    keys, values = k_ref[0], v_ref[0]
    total = jnp.zeros(queries.shape, jnp.float32)
    for head in range(LANES // HEAD_DIM):
        mask = head_mask(head)
        scores = dot_back((queries * mask).astype(jnp.bfloat16), keys)
        exped = jnp.exp(scores - jnp.max(scores, axis=1, keepdims=True))
        share = 1.0 / jnp.sum(exped, axis=1, keepdims=True)
        total = total + dot(exped.astype(jnp.bfloat16), values) * share * mask
    o_ref[0] = total


def attend_back_kernel(q_ref, k_ref, v_ref, o_ref, g_ref, dq_ref, dk_ref, dv_ref):
    scale = HEAD_DIM ** (-0.5)
    queries = q_ref[0].astype(jnp.float32) * scale
    grads = g_ref[0].astype(jnp.float32)
    keys, values = k_ref[0], v_ref[0]
    product = grads * o_ref[0]
    grad_q = jnp.zeros(queries.shape, jnp.float32)
    grad_k = jnp.zeros(keys.shape, jnp.float32)
    grad_v = jnp.zeros(keys.shape, jnp.float32)
    for head in range(LANES // HEAD_DIM):
        mask = head_mask(head)
        query = (queries * mask).astype(jnp.bfloat16)
        grad = (grads * mask).astype(jnp.bfloat16)
        scores = dot_back(keys, query)
        exped = jnp.exp(scores - jnp.max(scores, axis=0, keepdims=True))
        prob = exped * (1.0 / jnp.sum(exped, axis=0, keepdims=True))
        delta = lax.dot_general(
            jnp.broadcast_to(mask, (8, LANES)),
            product,
            (((1,), (1,)), ((), ())),
            precision=lax.Precision.HIGHEST,
            preferred_element_type=jnp.float32,
        )[:1]
        grad_score = (prob * (dot_back(values, grad) - delta)).astype(jnp.bfloat16)
        grad_v = grad_v + dot(prob.astype(jnp.bfloat16), grad)
        grad_k = grad_k + dot(grad_score, query)
        grad_q = grad_q + dot_rows(grad_score, keys) * (mask * scale)
    dq_ref[0] = grad_q.astype(jnp.bfloat16)
    dk_ref[0] = grad_k.astype(jnp.bfloat16)
    dv_ref[0] = grad_v.astype(jnp.bfloat16)


def attention_call(kernel, inputs, outputs, products):
    seqs, rows, width = inputs[0].shape
    keys = inputs[1].shape[1]

    def spec(array):
        return pl.BlockSpec((1, array.shape[1], LANES), lambda seq, part: (seq, 0, part))

    return pl.pallas_call(
        kernel,
        grid=(seqs, width // LANES),
        in_specs=[spec(item) for item in inputs],
        out_specs=[spec(item) for item in outputs],
        out_shape=outputs,
        compiler_params=pltpu.CompilerParams(vmem_limit_bytes=40 * 1024 * 1024),
        cost_estimate=pl.CostEstimate(
            flops=2 * products * seqs * rows * keys * width,
            bytes_accessed=sum(item.size * item.dtype.itemsize for item in inputs),
            transcendentals=seqs * rows * keys * width // HEAD_DIM,
        ),
    )(*inputs)


def per_device(
    tokens,
    w_qkv,
    b_query,
    b_value,
    w_attn_out,
    b_attn_out,
    norm1_gain,
    norm1_shift,
    w_up,
    b_up,
    w_down,
    b_down,
    norm2_gain,
    norm2_shift,
    d_out,
):
    count = lax.axis_size("fsdp")
    seq_local, block_rows, width = tokens.shape
    row_count = seq_local * block_rows
    tok_rows = tokens.reshape(row_count, width)
    vectors = (
        b_query,
        b_value,
        b_attn_out,
        norm1_gain,
        norm1_shift,
        b_up,
        b_down,
        norm2_gain,
        norm2_shift,
    )
    packed = lax.all_gather(jnp.concatenate(vectors), "fsdp", axis=0, tiled=False)
    spread, start = [], 0
    for item in vectors:
        size = item.shape[0]
        spread.append(packed[:, start : start + size].reshape(-1).astype(jnp.float32))
        start += size
    (
        query_bias,
        value_bias,
        out_bias,
        gain_one,
        shift_one,
        up_bias,
        down_bias,
        gain_two,
        shift_two,
    ) = spread
    bits = bits_of("fsdp")
    outer = bits - 1
    input_half = gather_hops(halves(w_qkv[None]), 0, outer)
    input_half, up_half, down_half = tie(
        input_half, halves(jnp.concatenate((w_attn_out, w_up), axis=1)[None]), halves(w_down[None])
    )
    input_proj = whole(gather_hops(input_half, outer, bits))
    token_blocks = gather_tokens(tok_rows)
    up_half = gather_hops(up_half, 0, outer)
    down_half = gather_hops(down_half, 0, outer)
    ctx_count = token_blocks.shape[0]
    score_scale = HEAD_DIM ** (-0.5)
    all_rows = reorder(token_blocks.reshape(ctx_count * row_count, width), count)
    own_rows = all_rows[:row_count]
    key_rows = ctx_count * block_rows

    def by_sequence(value):
        parts = value.reshape(ctx_count, seq_local, block_rows, width)
        return parts.transpose(1, 0, 2, 3).reshape(seq_local, key_rows, width)

    def by_block(value):
        parts = value.reshape(seq_local, ctx_count, block_rows, width)
        return parts.transpose(1, 0, 2, 3).reshape(ctx_count * row_count, width)

    queries = (dot(own_rows, input_proj[:, :width]) + query_bias).astype(jnp.bfloat16)
    queries = queries.reshape(seq_local, block_rows, width)
    key_part = by_sequence(dot(all_rows, input_proj[:, width : 2 * width]).astype(jnp.bfloat16))
    value_part = dot(all_rows, input_proj[:, 2 * width :]) + value_bias
    value_part = by_sequence(value_part.astype(jnp.bfloat16))
    mixed_out = attention_call(
        attend_kernel,
        (queries, key_part, value_part),
        (jax.ShapeDtypeStruct(queries.shape, jnp.float32),),
        2,
    )[0]
    up_half, down_half, mixed_out = tie(up_half, down_half, mixed_out)
    out_up = whole(gather_hops(up_half, outer, bits))
    down_weight = whole(gather_hops(down_half, outer, bits))
    out_weight, up_weight = out_up[:, :width], out_up[:, width:]
    attn_in = reorder(mixed_out.reshape(row_count, width).astype(jnp.bfloat16), count)
    attn_out = dot(attn_in, out_weight) + out_bias
    resid_one = tok_rows.astype(jnp.float32) + attn_out
    normed = layer_norm(resid_one, gain_one, shift_one)
    normed_low = reorder(normed.astype(jnp.bfloat16), count)
    hidden = dot(normed_low, up_weight) + up_bias
    activated = reorder(gelu_exact(hidden).astype(jnp.bfloat16), count)
    branch = dot(activated, down_weight) + down_bias
    resid_two = normed + branch
    result = layer_norm(resid_two, gain_two, shift_two)
    output = result.astype(jnp.bfloat16).reshape(seq_local, block_rows, width)
    cotangent = d_out.reshape(row_count, width).astype(jnp.float32)
    norm_pull = jax.vjp(layer_norm, resid_two, gain_two, shift_two)[1]
    grad_resid_two, grad_gain_two, grad_shift_two = norm_pull(cotangent)
    grad_branch = grad_resid_two.astype(jnp.bfloat16)
    down_blocks, grad_branch = tie(as_blocks(dot_rows(activated, grad_branch)), grad_branch)
    down_pair = scatter_core(down_blocks)
    grad_down_bias = jnp.sum(grad_branch.astype(jnp.float32), axis=0)
    grad_act = reorder(dot_back(grad_branch, down_weight), count)
    grad_hidden = jax.vjp(gelu_exact, hidden)[1](grad_act)[0].astype(jnp.bfloat16)
    up_blocks, grad_hidden = tie(as_blocks(dot_rows(normed_low, grad_hidden)), grad_hidden)
    up_pair = scatter_core(up_blocks)
    grad_up_bias = jnp.sum(grad_hidden.astype(jnp.float32), axis=0)
    down_pair, grad_hidden = tie(down_pair, grad_hidden)
    down_pair = scatter_hops(down_pair, 0, 1)
    grad_normed = grad_resid_two + reorder(dot_back(grad_hidden, up_weight), count)
    norm_pull_one = jax.vjp(layer_norm, resid_one, gain_one, shift_one)[1]
    grad_resid_one, grad_gain_one, grad_shift_one = norm_pull_one(grad_normed)
    grad_attn = grad_resid_one.astype(jnp.bfloat16)
    grad_out_weight = dot_rows(attn_in, grad_attn)
    up_pair, grad_attn = tie(up_pair, grad_attn)
    up_pair = scatter_hops(up_pair, 0, 1)
    grad_out_bias = jnp.sum(grad_attn.astype(jnp.float32), axis=0)
    grad_mixed = reorder(dot_back(grad_attn, out_weight).astype(jnp.bfloat16), count)
    down_pair, grad_mixed = tie(down_pair, grad_mixed)
    down_pair = scatter_hops(down_pair, 1, outer)
    grad_queries, grad_keys, grad_values = attention_call(
        attend_back_kernel,
        (queries, key_part, value_part, mixed_out, grad_mixed.reshape(queries.shape)),
        (
            jax.ShapeDtypeStruct(queries.shape, jnp.bfloat16),
            jax.ShapeDtypeStruct(key_part.shape, jnp.bfloat16),
            jax.ShapeDtypeStruct(key_part.shape, jnp.bfloat16),
        ),
        5,
    )
    up_pair, down_pair, grad_queries, grad_keys, grad_values = tie(
        up_pair, down_pair, grad_queries, grad_keys, grad_values
    )
    up_pair = scatter_hops(up_pair, 1, outer)
    down_own = ctx_hops(jnp.concatenate(down_pair, axis=2)[0], 0, 1)
    grad_queries = grad_queries.reshape(row_count, width)
    grad_keys, grad_values = by_block(grad_keys), by_block(grad_values)
    grad_kv = jnp.concatenate((grad_keys, grad_values), axis=1)
    grad_input_proj = jnp.concatenate(
        (dot_rows(own_rows, grad_queries), dot_rows(all_rows, grad_kv)), axis=1
    )
    grad_query_bias = jnp.sum(grad_queries.astype(jnp.float32), axis=0)
    grad_value_bias = jnp.sum(grad_values.astype(jnp.float32), axis=0)
    small = (
        grad_query_bias,
        grad_value_bias,
        grad_out_bias,
        grad_gain_one,
        grad_shift_one,
        grad_up_bias,
        grad_down_bias,
        grad_gain_two,
        grad_shift_two,
    )
    small_rows = jnp.concatenate([item.reshape(count, -1) for item in small], axis=1)
    small_size = small_rows.shape[1]
    me = lax.axis_index("fsdp")
    small_rows = jnp.concatenate(
        [lax.dynamic_slice_in_dim(small_rows, me ^ at, 1, 0) for at in range(count)], axis=0
    )
    own_width = width // count
    small_lines = -(-small_size // 128)
    small_rows = jnp.pad(small_rows, ((0, 0), (0, small_lines * 128 - small_size)))
    small_rows = small_rows.reshape(count, small_lines, 128).astype(jnp.bfloat16)
    small_rows = jnp.pad(small_rows, ((0, 0), (0, own_width - small_lines), (0, 0)))
    input_blocks = jnp.concatenate(
        (as_blocks(grad_input_proj), as_blocks(grad_out_weight), small_rows), axis=2
    )
    input_blocks, grad_kv = tie(input_blocks, grad_kv)
    input_pair = scatter_core(input_blocks)
    from_kv = dot_back(grad_kv, input_proj[:, width:])
    from_query = dot_back(grad_queries, input_proj[:, :width])
    from_kv = from_kv.astype(jnp.bfloat16).reshape(ctx_count, row_count, width)
    steps = 2 * bits_of("ctx")
    input_pair, from_kv, down_own, up_pair = tie(input_pair, from_kv, down_own, up_pair)
    input_pair = scatter_hops(input_pair, 0, 1)
    from_kv = scatter_tokens(from_kv)
    d_tokens = grad_resid_one + reorder(from_query + from_kv.astype(jnp.float32), count)
    down_own = ctx_hops(down_own, 1, 2)
    up_own = ctx_hops(fold(jnp.concatenate(up_pair, axis=2)[0], width), 0, 1)
    input_pair, down_own, up_own = tie(input_pair, down_own, up_own)
    input_pair = scatter_hops(input_pair, 1, outer)
    down_own = ctx_hops(down_own, 2, 3)
    up_own = ctx_hops(up_own, 1, 2)
    input_pair, down_own, up_own = tie(input_pair, down_own, up_own)
    input_own = jnp.concatenate(input_pair, axis=2)[0]
    extra = input_own[:small_lines, 4 * width :].reshape(-1)
    extra = jnp.pad(extra, (0, -extra.shape[0] % (16 * width))).reshape(-1, width)
    input_own = jnp.concatenate((fold(input_own[:, : 4 * width], width), extra), axis=0)
    for step in range(2, steps):
        input_own = ctx_hops(input_own, step - 2, step - 1)
        up_own = ctx_hops(up_own, step, step + 1)
        if step + 1 < steps:
            down_own = ctx_hops(down_own, step + 1, step + 2)
        input_own, up_own, down_own = tie(input_own, up_own, down_own)
    input_own = ctx_hops(input_own, steps - 2, steps).astype(jnp.float32)
    sum_down = down_own.astype(jnp.float32)
    sum_up = unfold(up_own.astype(jnp.float32), own_width)
    sum_input = unfold(input_own[: 3 * own_width], own_width)
    sum_out = input_own[3 * own_width : 4 * own_width]
    second_group = input_own
    small_own = second_group[4 * own_width :].reshape(-1)
    owned, start = [], 0
    for item in small:
        size = item.shape[0] // count
        owned.append(small_own[start : start + size])
        start += size
    return (
        output,
        d_tokens.reshape(seq_local, block_rows, width),
        sum_input,
        owned[0],
        owned[1],
        sum_out,
        owned[2],
        owned[3],
        owned[4],
        sum_up,
        owned[5],
        sum_down,
        owned[6],
        owned[7],
        owned[8],
    )


def solution(mesh):
    placed = (
        P("fsdp", "ctx", None),
        P("fsdp", None),
        P("fsdp"),
        P("fsdp"),
        P("fsdp", None),
        P("fsdp"),
        P("fsdp"),
        P("fsdp"),
        P("fsdp", None),
        P("fsdp"),
        P("fsdp", None),
        P("fsdp"),
        P("fsdp"),
        P("fsdp"),
        P("fsdp", "ctx", None),
    )
    return jax.shard_map(
        per_device,
        mesh=mesh,
        in_specs=placed,
        out_specs=(
            P("fsdp", "ctx", None),
            P("fsdp", "ctx", None),
            P("fsdp", None),
            P("fsdp"),
            P("fsdp"),
            P("fsdp", None),
            P("fsdp"),
            P("fsdp"),
            P("fsdp"),
            P("fsdp", None),
            P("fsdp"),
            P("fsdp", None),
            P("fsdp"),
            P("fsdp"),
            P("fsdp"),
        ),
        check_vma=False,
    )
```
